512 devices in a mesh: leaf: 2 (over core), row: 8 (over y_hi, x), col: 32 (over y_lo, z).
Axes of the slice: x: 4, y: 8 (y_hi: 2, y_lo: 4; y = y_hi * 4 + y_lo), z: 8, core: 2. Of those that a mesh axis runs over, the one named last changes fastest.
Arguments:
- front: float32 [4096, 32768], P('row', ('leaf', 'col')), may hold values from -6 to 6
- child_update: float32 [2, 4096, 16384], P('leaf', ('row', 'col')), may hold values from -6 to 6
- block_pattern: int32 [2, 16, 64], replicated, may hold values 0 or 1
- child_map: int32 [2, 64], replicated, may hold values from 0 to 127, as said below
- block_slot: int32 [128], replicated, may hold values from 0 to 127, each once
- diag_inverse: float32 [2, 256, 256], replicated, as said below
Outputs:
- updated: float32 [4096, 32768], P('row', ('leaf', 'col'))
The draws below stay inside these ranges and needn't reach their ends.
Inputs may be any that keep to these rules, and one draw needn't show every extreme that they name: `child_map`: each row lists 64 different parent blocks in increasing order and always includes blocks 0 and 127. `block_slot`: each slot once. `diag_inverse`: each matrix is lower triangular with a positive diagonal.
All inputs are finite; a program needn't handle non-finite values.
Results may differ from the reference program's by a relative error of at most 0.0001.
Values sent between devices are 32-bit elements; how exact they have to be, the bound alone decides.
A program may use at most 64 MiB of HBM per device.

```python
import math
import jax
import jax.numpy as jnp
from jax import lax

BLOCK = 256
FW = 32768
NB = 128
CW = 16384
CB = 64
SLAB = 4096
RBLK = 16
PANELS = 2


def draw_child_map(key, part):
    key = jax.random.fold_in(key, 11)
    listed = []
    for child_index in range(2):
        child_key = jax.random.fold_in(key, child_index)
        middle = jax.random.permutation(child_key, NB - 2)[:CB - 2] + 1
        chosen = jnp.concatenate([jnp.zeros((1,), jnp.int32), middle.astype(jnp.int32), jnp.full((1,), NB - 1, jnp.int32)])
        listed.append(jnp.sort(chosen))
    return jnp.stack(listed).astype(jnp.int32)


def draw_diag_inverse(key, part):
    key = jax.random.fold_in(key, 23)
    first_key, second_key = jax.random.split(key)
    diagonal = jnp.exp(jax.random.uniform(first_key, (PANELS, BLOCK), jnp.float32, math.log(0.05), math.log(0.1)))
    lower_part = jax.random.normal(second_key, (PANELS, BLOCK, BLOCK), jnp.float32) * 0.0018
    position = jnp.arange(BLOCK)
    strictly = position[:, None] > position[None, :]
    identity = (position[:, None] == position[None, :]).astype(jnp.float32)
    matrix = jnp.where(strictly[None], lower_part, 0.0) + diagonal[:, :, None] * identity[None]
    return matrix.astype(jnp.float32)


def plant(entries, own_key, least, high):
    place = [jax.random.randint(jax.random.fold_in(own_key, axis), (), 0, length) for axis, length in enumerate(entries.shape)]
    longest = entries.shape.index(max(entries.shape))
    next_to = place[:longest] + [(place[longest] + 1) % entries.shape[longest]] + place[longest + 1:]
    return entries.at[tuple(place)].set(least).at[tuple(next_to)].set(high)


def block_levels(own_key, shape, cuts, smallest, high):
    level = 1.0
    for dim, blocks in cuts:
        steps = jax.random.uniform(jax.random.fold_in(jax.random.fold_in(own_key, 6), dim), (blocks,), jnp.float32, smallest / len(cuts), high / len(cuts))
        level = level * jnp.repeat(jnp.exp(steps), shape[dim] // blocks).reshape((-1,) + (1,) * (len(shape) - 1 - dim))
    return level


def noise(rng, dims, deviation, bound, pieces=(), held_as=jnp.bfloat16):
    loudness = block_levels(rng, dims, pieces, -0.22, 0.18) if pieces else 1.0
    drawn = jax.random.normal(rng, dims, jnp.float32) * deviation * loudness
    return jnp.minimum(jnp.maximum(drawn, -bound), bound).astype(held_as)


def setup_inputs(seed: int = 0) -> dict:
    keys = jax.random.split(jax.random.key(seed), 7)
    return {
        "front": noise(keys[0], (SLAB, FW), 1.0, 6.0, ((0, 8), (1, 64)), jnp.float32),
        "child_update": noise(keys[1], (2, SLAB, CW), 1.0, 6.0, ((0, 2), (1, 256)), jnp.float32),
        "block_pattern": plant((jax.random.randint(keys[2], (2, RBLK, CB), 0, 4) < 3).astype(jnp.int32), jax.random.fold_in(keys[2], 1), 0, 1),
        "child_map": draw_child_map(jax.random.fold_in(keys[6], 71), 0),
        "block_slot": jax.random.permutation(keys[4], NB).astype(jnp.int32),
        "diag_inverse": draw_diag_inverse(jax.random.fold_in(keys[6], 71), 0),
    }


def reference(front, child_update, block_pattern, child_map, block_slot, diag_inverse):
    slab_rows, front_width = front.shape
    block_size = diag_inverse.shape[1]
    block_count = front_width // block_size
    child_blocks = child_map.shape[1]
    assembled = front.reshape(slab_rows, block_count, block_size)
    for child_index in range(child_update.shape[0]):
        pattern_float = block_pattern[child_index].astype(jnp.float32)
        contrib = child_update[child_index].reshape(slab_rows // block_size, block_size, child_blocks, block_size)
        contrib = contrib * pattern_float[:, None, :, None]
        target_slots = block_slot[child_map[child_index]]
        assembled = assembled.at[:, target_slots, :].add(contrib.reshape(slab_rows, child_blocks, block_size))
    working = assembled.reshape(slab_rows, front_width)
    slot_parent = jnp.zeros((block_count,), jnp.int32).at[block_slot].set(jnp.arange(block_count, dtype=jnp.int32))
    row_index = jnp.arange(slab_rows, dtype=jnp.int32)
    for panel in range(diag_inverse.shape[0]):
        inverse = diag_inverse[panel]
        column = lax.dynamic_slice_in_dim(working, (block_slot[panel] * block_size).astype(jnp.int32), block_size, 1)
        factored = jnp.dot(column, inverse.T, precision=lax.Precision.HIGHEST)
        pivot = jnp.dot(inverse, working[panel * block_size:(panel + 1) * block_size], precision=lax.Precision.HIGHEST)
        row_keep = row_index >= (panel + 1) * block_size
        col_keep = jnp.repeat(slot_parent > panel, block_size)
        update_mask = row_keep[:, None] & col_keep[None, :]
        product = jnp.dot(factored, pivot, precision=lax.Precision.HIGHEST)
        working = working - jnp.where(update_mask, product, jnp.float32(0.0))
    return working
```

```python
import jax
import jax.numpy as jnp
from jax import lax
from jax.experimental import pallas as pl
from jax.experimental.pallas import tpu as pltpu
from jax.sharding import PartitionSpec as P

MESH = pl.DeviceIdType.MESH
F32 = jnp.float32
BF16 = jnp.bfloat16
NX = 4
NZ = 8


def split(v):
    hi = v.astype(BF16)
    return hi, (v - hi.astype(F32)).astype(BF16)


def dot3(a, b, trans=False):
    dims = (((1,), (1 if trans else 0,)), ((), ()))
    ah, al = split(a)
    bh, bl = split(b)

    def d(u, v):
        return lax.dot_general(u, v, dims, preferred_element_type=F32)

    return d(ah, bh) + (d(ah, bl) + d(al, bh))


def make_kernel(ncol, nrow, b, nb, cb_count, sub):
    ny = ncol // NZ
    crow = ncol * sub // ny
    half = nb // 2

    def kernel(
        child_h, front_h, w_h, tab_s, slot_v, out_h,
        childs, blocks, front, w, maskp, pairf, colsum, yrecv, ysum, zrecv,
        cb2, sendbuf, recv, work, rbuf, f0, f1, g, e, p0, p1,
        loc_sem, pair_s, pair_r, a2a_s, a2a_r, y_s, y_r, z_s, z_r, d_s, d_r,
        ya_s, ya_r, yd_s, yd_r, za_s, za_r, rs_s, rs_r, out_sem,
    ):
        leaf = lax.axis_index("leaf")
        row = lax.axis_index("row")
        col = lax.axis_index("col")
        y, z = col // NZ, lax.rem(col, NZ)
        x, yh = lax.rem(row, NX), row // NX
        other = 1 - leaf
        own = leaf * ncol + col

        def rcopy(src, dst, ssem, rsem, **dev):
            return pltpu.make_async_remote_copy(
                src_ref=src, dst_ref=dst, send_sem=ssem, recv_sem=rsem,
                device_id=dev, device_id_type=MESH,
            )

        barrier = pltpu.get_barrier_semaphore()
        pl.semaphore_signal(barrier, inc=1, device_id={"leaf": other}, device_id_type=MESH)

        @pl.loop(1, nrow)
        def _(k):
            pl.semaphore_signal(
                barrier, inc=1, device_id={"row": lax.rem(row + k, nrow)}, device_id_type=MESH
            )

        @pl.loop(1, ncol)
        def _(k):
            pl.semaphore_signal(
                barrier, inc=1, device_id={"col": lax.rem(col + k, ncol)}, device_id_type=MESH
            )

        front_cp = pltpu.make_async_copy(front_h, front, loc_sem.at[0])
        child_cp = pltpu.make_async_copy(child_h.at[0], childs.at[leaf], loc_sem.at[1])
        w_cp = pltpu.make_async_copy(w_h, w, loc_sem.at[2])
        front_cp.start()
        child_cp.start()
        w_cp.start()

        pl.semaphore_wait(barrier, 1 + (nrow - 1) + (ncol - 1))

        child_rc = rcopy(child_h.at[0], childs.at[leaf], pair_s.at[0], pair_r.at[0], leaf=other)
        child_rc.start()

        pivot_slot = [slot_v[:, q : q + 1] for q in range(2)]

        def held(panel, t):
            at = jnp.where(panel == 0, pivot_slot[0], pivot_slot[1])
            return jnp.where(at == 2 * own + t, 1.0, 0.0).astype(F32)

        def masked(panel, i):
            v = front[pl.ds(i * 4, 4)].reshape(4 * sub, 2 * b)
            return v[:, :b] * held(panel, 0) + v[:, b:] * held(panel, 1)

        front_cp.wait()

        @pl.loop(0, ncol // 4)
        def _(i):
            maskp[pl.ds(i * 4 * sub, 4 * sub), :] = masked(other, i)

        mask_rc = rcopy(maskp, pairf, pair_s.at[1], pair_r.at[1], leaf=other)
        mask_rc.start()
        mask_rc.wait_recv()

        @pl.loop(0, ncol // 4)
        def _(i):
            at = pl.ds(i * 4 * sub, 4 * sub)
            colsum[at, :] = masked(leaf, i) + pairf[at, :]

        def y_rs(dy):
            to = lax.rem(y + dy, ny)
            return rcopy(
                colsum.at[pl.ds(to * crow, crow)], yrecv.at[dy - 1], y_s.at[dy - 1], y_r.at[dy - 1],
                col=to * NZ + z,
            )

        for dy in range(1, ny):
            y_rs(dy).start()

        child_cp.wait()
        child_rc.wait_recv()

        @pl.loop(0, cb_count)
        def _(j):
            lanes = pl.ds(pl.multiple_of(j * b, b), b)
            for c in range(2):
                blocks[c * cb_count + j] = childs[c, :, lanes]

        def piece(r0, lane_at):
            total = None
            for c in range(2):
                at = tab_s[r0 + c, lane_at]
                v = blocks[c * cb_count + jnp.maximum(at - 1, 0)] * jnp.minimum(at, 1).astype(F32)
                total = v if total is None else total + v
            return total

        def a2a(k):
            to = lax.rem(col + k, ncol)
            return rcopy(sendbuf.at[k], recv.at[col], a2a_s.at[k], a2a_r.at[k], col=to)

        for t in range(2):
            recv[col, :, t * b : (t + 1) * b] = piece(0, leaf * half + 2 * col + t)

        @pl.loop(1, ncol)
        def _(k):
            to = lax.rem(col + k, ncol)
            for t in range(2):
                sendbuf[k, :, t * b : (t + 1) * b] = piece(0, leaf * half + 2 * to + t)
            a2a(k).start()

        for dy in range(1, ny):
            y_rs(dy).wait_recv()
        ysum[...] = colsum[pl.ds(y * crow, crow), :] + yrecv[0] + yrecv[1] + yrecv[2]

        def z_rs(dz):
            to = lax.rem(z + dz, NZ)
            return rcopy(
                ysum.at[pl.ds(to * sub, sub)], zrecv.at[dz - 1], z_s.at[dz - 1], z_r.at[dz - 1],
                col=y * NZ + to,
            )

        for dz in range(1, NZ):
            z_rs(dz).start()

        cross = lambda k: jnp.where(lax.rem(k, 3) == 2, 3, lax.rem(k, 3))

        def relays(k):
            q = lax.rem(k, 3)
            odd = lax.rem(k, 2) == 1
            src = lax.rem(col - k + ncol, ncol)

            def to(n, dst):
                return rcopy(rbuf.at[src], rbuf.at[src], rs_s.at[n, k], rs_r.at[k], row=dst)

            out = [
                (row == 0, to(0, 1)),
                (row == 0, to(1, 3)),
                ((row == 0) & (q == 0), to(2, NX)),
                (((row == 1) & odd) | ((row == 3) & ~odd), to(0, 2)),
                (((row == 1) & (q == 1)) | ((row == 3) & (q == 2)), to(1, row + NX)),
            ]
            for dx in range(1, NX):
                out.append(((yh == 1) & (x == cross(k)), to(dx - 1, NX + lax.rem(x + dx, NX))))
            return out

        def relay(k):
            src = lax.rem(col - k + ncol, ncol)

            @pl.when(row == 0)
            def _():
                @pl.when(k > 0)
                def _():
                    a2a(k).wait_recv()

                v = front[src] + recv[src]
                work[src] = v
                rbuf[src] = v

            @pl.when(row != 0)
            def _():
                rcopy(rbuf.at[src], rbuf.at[src], rs_s.at[0, k], rs_r.at[k], row=0 * row).wait_recv()

            for cond, cp in relays(k):
                pl.when(cond)(cp.start)

        def relay_range(lo, hi):
            @pl.loop(lo, hi)
            def _(k):
                relay(k)

        relay_range(0, 6)

        for dz in range(1, NZ):
            z_rs(dz).wait_recv()
        mine = ysum[pl.ds(z * sub, sub), :] + piece(2, leaf)
        for dz in range(1, NZ):
            mine = mine + zrecv[dz - 1]
        cb2[leaf, y, z] = mine

        has_d = (y // (ny // 2)) == other
        de = ny + lax.rem(y, ny // 2)

        def y_ag(dy):
            to = lax.rem(y + dy, ny)
            return rcopy(
                cb2.at[leaf, y, z], cb2.at[leaf, y, z], ya_s.at[dy - 1], ya_r.at[dy - 1],
                col=to * NZ + z,
            )

        for dy in range(1, ny):
            y_ag(dy).start()

        def d_send(k):
            return rcopy(
                cb2.at[leaf, y, z], cb2.at[leaf, de, z], d_s.at[k - 1], d_r, row=lax.rem(row + k, nrow)
            )

        @pl.when(has_d & (row == 0))
        def _():
            cb2[leaf, de, z] = mine
            for k in range(1, nrow):
                d_send(k).start()

        relay_range(6, 14)

        def y_dag(dy):
            to = lax.rem(y + dy, ny)
            return rcopy(
                cb2.at[leaf, de, z], cb2.at[leaf, de, z], yd_s.at[dy - 1], yd_r.at[dy - 1],
                col=to * NZ + z,
            )

        @pl.when(has_d)
        def _():
            @pl.when(row != 0)
            def _():
                d_send(1).wait_recv()

            for dy in range(1, ny):
                y_dag(dy).start()

        for dy in range(1, ny):
            y_ag(dy).wait_recv()

            @pl.when((lax.rem(y - dy + ny, ny) // (ny // 2)) == other)
            def _():
                y_dag(dy).wait_recv()

        def z_ag(dz):
            to = lax.rem(z + dz, NZ)
            return rcopy(
                cb2.at[leaf, :, z], cb2.at[leaf, :, z], za_s.at[dz - 1], za_r.at[dz - 1],
                col=y * NZ + to,
            )

        for dz in range(1, NZ):
            z_ag(dz).start()

        relay_range(14, 24)

        for dz in range(1, NZ):
            z_ag(dz).wait_recv()
        col_rc = rcopy(cb2.at[leaf], cb2.at[leaf], pair_s.at[2], pair_r.at[2], leaf=other)
        col_rc.start()
        w_cp.wait()
        col_rc.wait_recv()

        e[...] = dot3(w[0], cb2[1, ny : ny + ny // 2].reshape(b, b))

        @pl.loop(0, ny // 2)
        def _(i):
            g[pl.ds(i * crow, crow), :] = dot3(cb2[0, ny + i].reshape(crow, b), w[0], True)

        @pl.loop(0, ny)
        def _(i):
            at = pl.ds(i * crow, crow)
            fa = dot3(cb2[0, i].reshape(crow, b), w[0], True)
            c1 = cb2[1, i].reshape(crow, b) - dot3(fa, e[...])
            fb = dot3(c1, w[1], True)
            f0[at, :] = jnp.where((row > 0) | (i >= ny // 2), fa, 0.0)
            f1[at, :] = jnp.where(row > 0, fb, 0.0)

        relay_range(24, ncol)

        @pl.when(row != 0)
        def _():
            @pl.loop(0, ncol)
            def _(k):
                src = lax.rem(col - k + ncol, ncol)

                @pl.when(k > 0)
                def _():
                    a2a(k).wait_recv()

                work[src] = front[src] + recv[src]

        pr = b // sub

        def out_copy(i):
            at = pl.ds(i * NZ, NZ)
            return pltpu.make_async_copy(work.at[at], out_h.at[at], out_sem.at[i])

        for t in range(2):
            lanes = slice(t * b, (t + 1) * b)
            pa = dot3(w[0], rbuf[0:pr, :, lanes].reshape(b, b))
            zz = rbuf[pr : 2 * pr, :, lanes].reshape(b, b) - dot3(g[...], pa)
            p0[:, lanes] = pa
            p1[:, lanes] = dot3(w[1], zz)

        @pl.loop(0, ny)
        def _(i):
            at = pl.ds(i * crow, crow)
            for t in range(2):
                lanes = slice(t * b, (t + 1) * b)
                s = 2 * own + t
                k0 = jnp.broadcast_to(pivot_slot[0], (crow, b)) != s
                k1 = k0 & (jnp.broadcast_to(pivot_slot[1], (crow, b)) != s)
                v = work[pl.ds(i * NZ, NZ), :, lanes].reshape(crow, b)
                v = v - jnp.where(k0, dot3(f0[at, :], p0[:, lanes]), 0.0)
                v = v - jnp.where(k1, dot3(f1[at, :], p1[:, lanes]), 0.0)
                work[pl.ds(i * NZ, NZ), :, lanes] = v.reshape(NZ, sub, b)
            out_copy(i).start()

        child_rc.wait_send()
        mask_rc.wait_send()
        col_rc.wait_send()
        for dy in range(1, ny):
            y_rs(dy).wait_send()
            y_ag(dy).wait_send()
        for dz in range(1, NZ):
            z_rs(dz).wait_send()
            z_ag(dz).wait_send()

        @pl.when(has_d)
        def _():
            for dy in range(1, ny):
                y_dag(dy).wait_send()

            @pl.when(row == 0)
            def _():
                for k in range(1, nrow):
                    d_send(k).wait_send()

        @pl.loop(1, ncol)
        def _(k):
            a2a(k).wait_send()

        @pl.loop(0, ncol)
        def _(k):
            for cond, cp in relays(k):
                pl.when(cond)(cp.wait_send)

        @pl.loop(0, ny)
        def _(i):
            out_copy(i).wait()

    dma = pltpu.SemaphoreType.DMA
    width = 2 * b
    rows = ncol * sub
    scratch = [
        pltpu.VMEM((2, sub, cb_count * b), F32),
        pltpu.VMEM((2 * cb_count, sub, b), F32),
        pltpu.VMEM((ncol, sub, width), F32),
        pltpu.VMEM((2, b, b), F32),
        pltpu.VMEM((rows, b), F32),
        pltpu.VMEM((rows, b), F32),
        pltpu.VMEM((rows, b), F32),
        pltpu.VMEM((ny - 1, crow, b), F32),
        pltpu.VMEM((crow, b), F32),
        pltpu.VMEM((NZ - 1, sub, b), F32),
        pltpu.VMEM((2, ny + ny // 2, NZ, sub, b), F32),
        pltpu.VMEM((ncol, sub, width), F32),
        pltpu.VMEM((ncol, sub, width), F32),
        pltpu.VMEM((ncol, sub, width), F32),
        pltpu.VMEM((ncol, sub, width), F32),
        pltpu.VMEM((rows, b), F32),
        pltpu.VMEM((rows, b), F32),
        pltpu.VMEM((b, b), F32),
        pltpu.VMEM((b, b), F32),
        pltpu.VMEM((b, width), F32),
        pltpu.VMEM((b, width), F32),
        dma((4,)), dma((3,)), dma((3,)), dma((ncol,)), dma((ncol,)),
        dma((ny - 1,)), dma((ny - 1,)), dma((NZ - 1,)), dma((NZ - 1,)),
        dma((nrow - 1,)), dma,
        dma((ny - 1,)), dma((ny - 1,)), dma((ny - 1,)), dma((ny - 1,)),
        dma((NZ - 1,)), dma((NZ - 1,)), dma((3, ncol)), dma((ncol,)), dma((ny,)),
    ]
    return kernel, scratch


def on_device(front, child_update, block_pattern, child_map, block_slot, diag_inverse):
    rows, width = front.shape
    b = diag_inverse.shape[1]
    sub = child_update.shape[1]
    nb = block_slot.shape[0]
    cb_count = child_map.shape[1]
    ncol, nrow = lax.axis_size("col"), lax.axis_size("row")
    kernel, scratch = make_kernel(ncol, nrow, b, nb, cb_count, sub)
    row_block = (lax.axis_index("row") * ncol + lax.axis_index("col")) * sub // b
    present = lax.dynamic_index_in_dim(block_pattern, row_block, 1, keepdims=False)
    code = (present * (jnp.arange(cb_count, dtype=jnp.int32) + 1))[:, :, None]
    ids = jnp.arange(nb, dtype=jnp.int32)
    parents = child_map[:, :, None]
    slots = jnp.sum(jnp.where(parents == ids, block_slot, 0), axis=2, keepdims=True)
    tables = jnp.concatenate(
        [jnp.sum(jnp.where(key == ids, code, 0), axis=1) for key in (slots, parents)]
    )
    hbm = pl.BlockSpec(memory_space=pl.ANY)
    vmem = pl.BlockSpec(memory_space=pltpu.VMEM)
    out = pl.pallas_call(
        kernel,
        out_shape=jax.ShapeDtypeStruct((ncol, sub, width), F32),
        in_specs=[hbm, hbm, hbm, pl.BlockSpec(memory_space=pltpu.SMEM), vmem],
        out_specs=hbm,
        scratch_shapes=scratch,
        compiler_params=pltpu.CompilerParams(
            collective_id=0, has_side_effects=True, vmem_limit_bytes=40 << 20
        ),
        cost_estimate=pl.CostEstimate(
            flops=6 * 22 * b * b * b, bytes_accessed=12 * rows * width, transcendentals=0
        ),
    )(
        child_update, front.reshape(ncol, sub, width), diag_inverse,
        tables, block_slot.reshape(1, nb),
    )
    return out.reshape(rows, width)


def solution(mesh):
    return jax.shard_map(
        on_device,
        mesh=mesh,
        in_specs=(P("row", ("leaf", "col")), P("leaf", ("row", "col"), None), P(), P(), P(), P()),
        out_specs=P("row", ("leaf", "col")),
        check_vma=False,
    )
```

```python
import jax
import jax.numpy as jnp
from jax import lax
from jax.experimental import pallas as pl
from jax.experimental.pallas import tpu as pltpu
from jax.sharding import PartitionSpec as P

MESH = pl.DeviceIdType.MESH
F32 = jnp.float32
BF16 = jnp.bfloat16
NX = 4
NZ = 8
UNITS = 8
TREE = (0, 0, 0, 0, 0, 0, 1, 1, 0, 0)
CROSS = (2, 2, 1, 3, 1, 3, 0, 0, 1, 3)
FIRST = ((0,), (1,), (2, 3, 4), (8, 9), (5, 6, 7))
OTHER = ((), (), (0, 1, 2, 3), (8, 9), (4, 5, 6, 7))


def split(v):
    hi = v.astype(BF16)
    return hi, (v - hi.astype(F32)).astype(BF16)


def dot3(a, b, trans=False):
    dims = (((1,), (1 if trans else 0,)), ((), ()))
    ah, al = split(a)
    bh, bl = split(b)

    def d(u, v):
        return lax.dot_general(u, v, dims, preferred_element_type=F32)

    return d(ah, bh) + (d(ah, bl) + d(al, bh))


def make_kernel(ncol, nrow, b, nb, cb_count, sub):
    ny = ncol // NZ
    crow = ncol * sub // ny
    per = ncol // UNITS
    half = nb // 2

    def kernel(
        child_h, front_h, w_h, tab_s, slot_v, out_h,
        childs, blocks, front, w, maskp, pairf, colsum, ybig, ysum, zsmall, zbig, zsum, ysmall,
        cb2, dbuf, sendbuf, recv, work, rbuf, pivots, f0, f1, g, e, p0, p1,
        loc_sem, pair_s, pair_r, a2a_s, a2a_r, y_s, y_r, z_s, z_r,
        ya_s, ya_r, za_s, za_r, rs_s, rs_r, out_sem,
    ):
        leaf = lax.axis_index("leaf")
        row = lax.axis_index("row")
        col = lax.axis_index("col")
        y, z = col // NZ, lax.rem(col, NZ)
        other = 1 - leaf
        own = leaf * ncol + col

        def rcopy(src, dst, ssem, rsem, **dev):
            return pltpu.make_async_remote_copy(
                src_ref=src, dst_ref=dst, send_sem=ssem, recv_sem=rsem,
                device_id=dev, device_id_type=MESH,
            )

        barrier = pltpu.get_barrier_semaphore()
        pl.semaphore_signal(barrier, inc=1, device_id={"leaf": other}, device_id_type=MESH)

        @pl.loop(1, nrow)
        def _(k):
            pl.semaphore_signal(
                barrier, inc=1, device_id={"row": lax.rem(row + k, nrow)}, device_id_type=MESH
            )

        @pl.loop(1, ncol)
        def _(k):
            pl.semaphore_signal(
                barrier, inc=1, device_id={"col": lax.rem(col + k, ncol)}, device_id_type=MESH
            )

        front_cp = pltpu.make_async_copy(front_h, front, loc_sem.at[0])
        child_cp = pltpu.make_async_copy(child_h.at[0], childs.at[leaf], loc_sem.at[1])
        w_cp = pltpu.make_async_copy(w_h, w, loc_sem.at[2])
        front_cp.start()
        child_cp.start()
        w_cp.start()

        pivot_slot = [slot_v[:, q : q + 1] for q in range(2)]

        def held(panel, t):
            at = jnp.where(panel == 0, pivot_slot[0], pivot_slot[1])
            return jnp.where(at == 2 * own + t, 1.0, 0.0).astype(F32)

        def masked(panel, i):
            v = front[pl.ds(i * NZ, NZ)].reshape(crow, 2 * b)
            return (v[:, :b] * held(panel, 0) + v[:, b:] * held(panel, 1)).reshape(NZ, sub, b)

        front_cp.wait()

        @pl.loop(0, ny)
        def _(i):
            maskp[i] = masked(other, i)

        mask_rc = rcopy(maskp, pairf, pair_s.at[1], pair_r.at[1], leaf=other)
        child_rc = rcopy(child_h.at[0], childs.at[leaf], pair_s.at[0], pair_r.at[0], leaf=other)
        pl.semaphore_wait(barrier, 1 + (nrow - 1) + (ncol - 1))
        mask_rc.start()
        child_rc.start()
        mask_rc.wait_recv()

        @pl.loop(0, ny)
        def _(i):
            colsum[i] = masked(leaf, i) + pairf[i]

        def y_to(dy):
            return lax.rem(y + dy, ny)

        def z_to(dz):
            return lax.rem(z + dz, NZ)

        def over_y(src, dst, ssem, rsem):
            return [
                rcopy(src(y_to(d)), dst(d - 1), ssem.at[d - 1], rsem.at[d - 1], col=y_to(d) * NZ + z)
                for d in range(1, ny)
            ]

        def over_z(src, dst, ssem, rsem):
            return [
                rcopy(src(z_to(d)), dst(d - 1), ssem.at[d - 1], rsem.at[d - 1], col=y * NZ + z_to(d))
                for d in range(1, NZ)
            ]

        def column_steps(which):
            if which == 0:
                return (
                    lambda: over_y(lambda t: colsum.at[t], lambda i: ybig.at[i], y_s, y_r),
                    lambda: over_z(lambda t: ysum.at[t], lambda i: zsmall.at[i], z_s, z_r),
                    lambda: over_z(lambda t: cb2.at[0, y, z], lambda i: cb2.at[0, y, z], za_s, za_r),
                    lambda: over_y(lambda t: cb2.at[0, y], lambda i: cb2.at[0, y], ya_s, ya_r),
                )
            return (
                lambda: over_z(lambda t: colsum.at[:, t], lambda i: zbig.at[i], z_s, z_r),
                lambda: over_y(lambda t: zsum.at[t], lambda i: ysmall.at[i], y_s, y_r),
                lambda: over_y(lambda t: cb2.at[1, y, z], lambda i: cb2.at[1, y, z], ya_s, ya_r),
                lambda: over_z(lambda t: cb2.at[1, :, z], lambda i: cb2.at[1, :, z], za_s, za_r),
            )

        def each_leaf(f):
            for which in range(2):
                pl.when(leaf == which)(lambda which=which: f(which, column_steps(which)))

        def start(copies):
            for cp in copies:
                cp.start()

        def arrive(copies):
            for cp in copies:
                cp.wait_recv()

        @each_leaf
        def _(which, steps):
            start(steps[0]())

        child_cp.wait()
        child_rc.wait_recv()

        @pl.loop(0, cb_count)
        def _(j):
            lanes = pl.ds(pl.multiple_of(j * b, b), b)
            for c in range(2):
                blocks[c * cb_count + j] = childs[c, :, lanes]

        def piece(r0, lane_at):
            total = None
            for c in range(2):
                at = tab_s[r0 + c, lane_at]
                v = blocks[c * cb_count + jnp.maximum(at - 1, 0)] * jnp.minimum(at, 1).astype(F32)
                total = v if total is None else total + v
            return total

        def a2a(k):
            to = lax.rem(col + k, ncol)
            return rcopy(sendbuf.at[k], recv.at[k], a2a_s.at[k], a2a_r.at[k], col=to)

        def back(k):
            return lax.rem(col - k + ncol, ncol)

        for t in range(2):
            recv[0, :, t * b : (t + 1) * b] = piece(0, leaf * half + 2 * col + t)

        @pl.loop(1, ncol)
        def _(k):
            to = lax.rem(col + k, ncol)
            for t in range(2):
                sendbuf[k, :, t * b : (t + 1) * b] = piece(0, leaf * half + 2 * to + t)
            a2a(k).start()

        def edges(u):
            rise = u % 2 == 0
            if TREE[u]:
                out = [(0, 1), (0, 3), (1, 2) if rise else (3, 2)]
            else:
                out = [(0, 1), (1, 2), (2, 3)] if rise else [(0, 3), (3, 2), (2, 1)]
            at = CROSS[u]
            out.append((at, at + NX))
            return out + [(at + NX, (at + d) % NX + NX) for d in range(1, NX)]

        def unit_ref(u):
            if u < UNITS:
                return rbuf.at[pl.ds(u * per, per)]
            return dbuf.at[leaf, u - UNITS]

        def unit_sends(u, src):
            return [
                rcopy(unit_ref(u), unit_ref(u), rs_s.at[n, u], rs_r.at[u], row=dst)
                for n, dst in enumerate(d for s, d in edges(u) if s == src)
            ]

        def unit_wait(u):
            rcopy(unit_ref(u), unit_ref(u), rs_s.at[0, u], rs_r.at[u], row=row).wait_recv()

        def relay(u, rows_of):
            for src in sorted({s for s, _ in edges(u) if (s == 0) == rows_of}):

                @pl.when(row == src)
                def _():
                    if src:
                        unit_wait(u)
                    elif u < UNITS:

                        @pl.loop(u * per, (u + 1) * per)
                        def _(k):
                            if u:
                                a2a(k).wait_recv()
                            else:
                                pl.when(k > 0)(lambda: a2a(k).wait_recv())
                            v = front[back(k)] + recv[k]
                            work[back(k)] = v
                            rbuf[k] = v
                    else:
                        dbuf[leaf, u - UNITS] = cb2[leaf, other * (ny // 2) + u - UNITS]
                    start(unit_sends(u, src))

        def do_relays(name):
            for u in FIRST[name]:
                relay(u, True)
            for u in OTHER[name]:
                relay(u, False)

        @each_leaf
        def _(which, steps):
            arrive(steps[0]())
            if which == 0:
                ysum[...] = colsum[y] + ybig[0] + ybig[1] + ybig[2]
            else:
                total = colsum[:, z]
                for d in range(NZ - 1):
                    total = total + zbig[d]
                zsum[...] = total
            start(steps[1]())

        do_relays(0)

        @each_leaf
        def _(which, steps):
            arrive(steps[1]())
            part, small, n = (ysum[z], zsmall, NZ - 1) if which == 0 else (zsum[y], ysmall, ny - 1)
            part = part + piece(2, which)
            for d in range(n):
                part = part + small[d]
            cb2[which, y, z] = part
            start(steps[2]())

        do_relays(1)

        @each_leaf
        def _(which, steps):
            arrive(steps[2]())
            start(steps[3]())

        do_relays(2)

        @each_leaf
        def _(which, steps):
            arrive(steps[3]())

        col_rc = rcopy(cb2.at[leaf], cb2.at[leaf], pair_s.at[2], pair_r.at[2], leaf=other)
        col_rc.start()
        do_relays(3)

        def leaf_only(f):
            for u in range(UNITS, UNITS + 2):
                for r in range(1, 2 * NX):
                    if r not in {s for s, _ in edges(u)}:
                        pl.when(row == r)(lambda u=u: f(u))

        do_relays(4)
        leaf_only(unit_wait)
        d_rc = rcopy(dbuf.at[leaf], dbuf.at[leaf], pair_s.at[3], pair_r.at[3], leaf=other)
        d_rc.start()
        w_cp.wait()
        col_rc.wait_recv()
        d_rc.wait_recv()

        e[...] = dot3(w[0], dbuf[1].reshape(b, b))

        @pl.loop(0, ny // 2)
        def _(i):
            g[pl.ds(i * crow, crow), :] = dot3(dbuf[0, i].reshape(crow, b), w[0], True)

        @pl.loop(0, ny)
        def _(i):
            at = pl.ds(i * crow, crow)
            fa = dot3(cb2[0, i].reshape(crow, b), w[0], True)
            c1 = cb2[1, i].reshape(crow, b) - dot3(fa, e[...])
            fb = dot3(c1, w[1], True)
            f0[at, :] = jnp.where((row > 0) | (i >= ny // 2), fa, 0.0)
            f1[at, :] = jnp.where(row > 0, fb, 0.0)

        @pl.when(row != 0)
        def _():
            @pl.loop(0, ncol)
            def _(k):
                pl.when(k > 0)(lambda: a2a(k).wait_recv())
                work[back(k)] = front[back(k)] + recv[k]

        for u in range(UNITS):
            for r in range(1, 2 * NX):
                if r not in {s for s, _ in edges(u)}:
                    pl.when(row == r)(lambda u=u: unit_wait(u))

        @pl.loop(0, ncol)
        def _(k):
            pivots[back(k)] = rbuf[k]

        pr = b // sub

        def out_copy(i):
            at = pl.ds(i * NZ, NZ)
            return pltpu.make_async_copy(work.at[at], out_h.at[at], out_sem.at[i])

        for t in range(2):
            lanes = slice(t * b, (t + 1) * b)
            pa = dot3(w[0], pivots[0:pr, :, lanes].reshape(b, b))
            zz = pivots[pr : 2 * pr, :, lanes].reshape(b, b) - dot3(g[...], pa)
            p0[:, lanes] = pa
            p1[:, lanes] = dot3(w[1], zz)
        @pl.loop(0, ny)
        def _(i):
            at = pl.ds(i * crow, crow)
            for t in range(2):
                lanes = slice(t * b, (t + 1) * b)
                s = 2 * own + t
                k0 = jnp.broadcast_to(pivot_slot[0], (crow, b)) != s
                k1 = k0 & (jnp.broadcast_to(pivot_slot[1], (crow, b)) != s)
                v = work[pl.ds(i * NZ, NZ), :, lanes].reshape(crow, b)
                v = v - jnp.where(k0, dot3(f0[at, :], p0[:, lanes]), 0.0)
                v = v - jnp.where(k1, dot3(f1[at, :], p1[:, lanes]), 0.0)
                work[pl.ds(i * NZ, NZ), :, lanes] = v.reshape(NZ, sub, b)
            out_copy(i).start()

        for cp in (child_rc, mask_rc, col_rc, d_rc):
            cp.wait_send()

        @each_leaf
        def _(which, steps):
            for step in steps:
                for cp in step():
                    cp.wait_send()

        @pl.loop(1, ncol)
        def _(k):
            a2a(k).wait_send()

        for u in range(UNITS + 2):
            for src in sorted({s for s, _ in edges(u)}):

                @pl.when(row == src)
                def _():
                    for cp in unit_sends(u, src):
                        cp.wait_send()

        @pl.loop(0, ny)
        def _(i):
            out_copy(i).wait()

    dma = pltpu.SemaphoreType.DMA
    width = 2 * b
    rows = ncol * sub
    scratch = [
        pltpu.VMEM((2, sub, cb_count * b), F32),
        pltpu.VMEM((2 * cb_count, sub, b), F32),
        pltpu.VMEM((ncol, sub, width), F32),
        pltpu.VMEM((2, b, b), F32),
        pltpu.VMEM((ny, NZ, sub, b), F32),
        pltpu.VMEM((ny, NZ, sub, b), F32),
        pltpu.VMEM((ny, NZ, sub, b), F32),
        pltpu.VMEM((ny - 1, NZ, sub, b), F32),
        pltpu.VMEM((NZ, sub, b), F32),
        pltpu.VMEM((NZ - 1, sub, b), F32),
        pltpu.VMEM((NZ - 1, ny, sub, b), F32),
        pltpu.VMEM((ny, sub, b), F32),
        pltpu.VMEM((ny - 1, sub, b), F32),
        pltpu.VMEM((2, ny, NZ, sub, b), F32),
        pltpu.VMEM((2, ny // 2, NZ, sub, b), F32),
        pltpu.VMEM((ncol, sub, width), F32),
        pltpu.VMEM((ncol, sub, width), F32),
        pltpu.VMEM((ncol, sub, width), F32),
        pltpu.VMEM((ncol, sub, width), F32),
        pltpu.VMEM((ncol, sub, width), F32),
        pltpu.VMEM((rows, b), F32),
        pltpu.VMEM((rows, b), F32),
        pltpu.VMEM((b, b), F32),
        pltpu.VMEM((b, b), F32),
        pltpu.VMEM((b, width), F32),
        pltpu.VMEM((b, width), F32),
        dma((4,)), dma((4,)), dma((4,)), dma((ncol,)), dma((ncol,)),
        dma((ny - 1,)), dma((ny - 1,)), dma((NZ - 1,)), dma((NZ - 1,)),
        dma((ny - 1,)), dma((ny - 1,)), dma((NZ - 1,)), dma((NZ - 1,)),
        dma((3, UNITS + 2)), dma((UNITS + 2,)), dma((ny,)),
    ]
    return kernel, scratch


def on_device(front, child_update, block_pattern, child_map, block_slot, diag_inverse):
    rows, width = front.shape
    b = diag_inverse.shape[1]
    sub = child_update.shape[1]
    nb = block_slot.shape[0]
    cb_count = child_map.shape[1]
    ncol, nrow = lax.axis_size("col"), lax.axis_size("row")
    kernel, scratch = make_kernel(ncol, nrow, b, nb, cb_count, sub)
    row_block = (lax.axis_index("row") * ncol + lax.axis_index("col")) * sub // b
    present = lax.dynamic_index_in_dim(block_pattern, row_block, 1, keepdims=False)
    code = (present * (jnp.arange(cb_count, dtype=jnp.int32) + 1))[:, :, None]
    ids = jnp.arange(nb, dtype=jnp.int32)
    parents = child_map[:, :, None]
    slots = jnp.sum(jnp.where(parents == ids, block_slot, 0), axis=2, keepdims=True)
    tables = jnp.concatenate(
        [jnp.sum(jnp.where(key == ids, code, 0), axis=1) for key in (slots, parents)]
    )
    hbm = pl.BlockSpec(memory_space=pl.ANY)
    vmem = pl.BlockSpec(memory_space=pltpu.VMEM)
    out = pl.pallas_call(
        kernel,
        out_shape=jax.ShapeDtypeStruct((ncol, sub, width), F32),
        in_specs=[hbm, hbm, hbm, pl.BlockSpec(memory_space=pltpu.SMEM), vmem],
        out_specs=hbm,
        scratch_shapes=scratch,
        compiler_params=pltpu.CompilerParams(
            collective_id=0, has_side_effects=True, vmem_limit_bytes=60 << 20
        ),
        cost_estimate=pl.CostEstimate(
            flops=6 * 22 * b * b * b, bytes_accessed=12 * rows * width, transcendentals=0
        ),
    )(
        child_update, front.reshape(ncol, sub, width), diag_inverse,
        tables, block_slot.reshape(1, nb),
    )
    return out.reshape(rows, width)


def solution(mesh):
    return jax.shard_map(
        on_device,
        mesh=mesh,
        in_specs=(P("row", ("leaf", "col")), P("leaf", ("row", "col"), None), P(), P(), P(), P()),
        out_specs=P("row", ("leaf", "col")),
        check_vma=False,
    )
```

```python
import jax
import jax.numpy as jnp
from jax import lax
from jax.experimental import pallas as pl
from jax.experimental.pallas import tpu as pltpu
from jax.sharding import PartitionSpec as P

MESH = pl.DeviceIdType.MESH
F32 = jnp.float32
BF16 = jnp.bfloat16
NX = 4
NZ = 8


def split(v):
    hi = v.astype(BF16)
    return hi, (v - hi.astype(F32)).astype(BF16)


def dot3(a, b, trans=False):
    dims = (((1,), (1 if trans else 0,)), ((), ()))
    ah, al = split(a)
    bh, bl = split(b)

    def d(u, v):
        return lax.dot_general(u, v, dims, preferred_element_type=F32)

    return d(ah, bh) + (d(ah, bl) + d(al, bh))


def make_kernel(ncol, nrow, b, nb, cb_count, sub):
    ny = ncol // NZ
    crow = ncol * sub // ny
    fold = ncol // NX
    half = nb // 2

    def kernel(
        child_h, front_h, w_h, tab_s, slot_v, out_h,
        childs, blocks, front, w, maskp, pairf, colsum, ybig, ysum, zsmall, zbig, zsum, ysmall,
        cb2, dbuf, sendbuf, recv, work, stage, front_x, rq, pivots, f0, f1, g, e, p0, p1,
        loc_sem, pair_s, pair_r, a2a_s, a2a_r, y_s, y_r, z_s, z_r,
        ya_s, ya_r, za_s, za_r, rs_s, rs_r, rf_s, rf_r, rl_s, rl_r, rq_s, rq_r, d_s, d_r, dg_s, dg_r, dh_s, dh_r, out_sem,
    ):
        leaf = lax.axis_index("leaf")
        row = lax.axis_index("row")
        col = lax.axis_index("col")
        y, z = col // NZ, lax.rem(col, NZ)
        other = 1 - leaf
        own = leaf * ncol + col

        def rcopy(src, dst, ssem, rsem, **dev):
            return pltpu.make_async_remote_copy(
                src_ref=src, dst_ref=dst, send_sem=ssem, recv_sem=rsem,
                device_id=dev, device_id_type=MESH,
            )

        barrier = pltpu.get_barrier_semaphore()
        pl.semaphore_signal(barrier, inc=1, device_id={"leaf": other}, device_id_type=MESH)

        @pl.loop(1, nrow)
        def _(k):
            pl.semaphore_signal(
                barrier, inc=1, device_id={"row": lax.rem(row + k, nrow)}, device_id_type=MESH
            )

        @pl.loop(1, ncol)
        def _(k):
            pl.semaphore_signal(
                barrier, inc=1, device_id={"col": lax.rem(col + k, ncol)}, device_id_type=MESH
            )

        front_cp = pltpu.make_async_copy(front_h, front, loc_sem.at[0])
        child_cp = pltpu.make_async_copy(child_h.at[0], childs.at[leaf], loc_sem.at[1])
        w_cp = pltpu.make_async_copy(w_h, w, loc_sem.at[2])
        front_cp.start()
        child_cp.start()
        w_cp.start()

        pivot_slot = [slot_v[:, q : q + 1] for q in range(2)]

        def held(panel, t):
            at = jnp.where(panel == 0, pivot_slot[0], pivot_slot[1])
            return jnp.where(at == 2 * own + t, 1.0, 0.0).astype(F32)

        def masked(panel, i):
            v = front[pl.ds(i * (NZ // NX), NZ // NX)].reshape(crow, 2 * b)
            return (v[:, :b] * held(panel, 0) + v[:, b:] * held(panel, 1)).reshape(NZ, sub, b)

        front_cp.wait()

        @pl.loop(0, ny)
        def _(i):
            maskp[i] = masked(other, i)

        mask_rc = rcopy(maskp, pairf, pair_s.at[1], pair_r.at[1], leaf=other)
        child_rc = rcopy(child_h.at[0], childs.at[leaf], pair_s.at[0], pair_r.at[0], leaf=other)
        pl.semaphore_wait(barrier, 1 + (nrow - 1) + (ncol - 1))
        mask_rc.start()
        child_rc.start()

        def lot(k):
            return lax.rem(col - k + ncol, NX)

        def front_to(k):
            return rcopy(front.at[:, lot(k)], front_x, rf_s.at[k - 1], rf_r, row=k)

        mask_rc.wait_recv()

        @pl.loop(0, ny)
        def _(i):
            colsum[i] = masked(leaf, i) + pairf[i]

        def y_to(dy):
            return lax.rem(y + dy, ny)

        def z_to(dz):
            return lax.rem(z + dz, NZ)

        def over_y(src, dst, ssem, rsem):
            return [
                rcopy(src(y_to(d)), dst(d - 1), ssem.at[d - 1], rsem.at[d - 1], col=y_to(d) * NZ + z)
                for d in range(1, ny)
            ]

        def over_z(src, dst, ssem, rsem):
            return [
                rcopy(src(z_to(d)), dst(d - 1), ssem.at[d - 1], rsem.at[d - 1], col=y * NZ + z_to(d))
                for d in range(1, NZ)
            ]

        def column_steps(which):
            if which == 0:
                return (
                    lambda: over_y(lambda t: colsum.at[t], lambda i: ybig.at[i], y_s, y_r),
                    lambda: over_z(lambda t: ysum.at[t], lambda i: zsmall.at[i], z_s, z_r),
                    lambda: over_z(lambda t: cb2.at[0, y, z], lambda i: cb2.at[0, y, z], za_s, za_r),
                    lambda: over_y(lambda t: cb2.at[0, y], lambda i: cb2.at[0, y], ya_s, ya_r),
                )
            return (
                lambda: over_z(lambda t: colsum.at[:, t], lambda i: zbig.at[i], z_s, z_r),
                lambda: over_y(lambda t: zsum.at[t], lambda i: ysmall.at[i], y_s, y_r),
                lambda: over_y(lambda t: cb2.at[1, y, z], lambda i: cb2.at[1, y, z], ya_s, ya_r),
                lambda: over_z(lambda t: cb2.at[1, :, z], lambda i: cb2.at[1, :, z], za_s, za_r),
            )

        def each_leaf(f):
            for which in range(2):
                pl.when(leaf == which)(lambda which=which: f(which, column_steps(which)))

        def start(copies):
            for cp in copies:
                cp.start()

        def arrive(copies):
            for cp in copies:
                cp.wait_recv()

        @each_leaf
        def _(which, steps):
            start(steps[0]())

        child_cp.wait()
        child_rc.wait_recv()

        @pl.loop(0, cb_count)
        def _(j):
            lanes = pl.ds(pl.multiple_of(j * b, b), b)
            for c in range(2):
                blocks[c * cb_count + j] = childs[c, :, lanes]

        def piece(r0, lane_at):
            total = None
            for c in range(2):
                at = tab_s[r0 + c, lane_at]
                v = blocks[c * cb_count + jnp.maximum(at - 1, 0)] * jnp.minimum(at, 1).astype(F32)
                total = v if total is None else total + v
            return total

        def slot_of(k):
            return lax.rem(k, NX) * fold + k // NX

        def a2a(k):
            to = lax.rem(col + k, ncol)
            return rcopy(sendbuf.at[slot_of(k)], recv.at[k], a2a_s.at[k], a2a_r.at[k], col=to)

        def back(k):
            return lax.rem(col - k + ncol, ncol)

        def build(k):
            to = lax.rem(col + k, ncol)
            for t in range(2):
                sendbuf[slot_of(k), :, t * b : (t + 1) * b] = piece(0, leaf * half + 2 * to + t)

        def lot_to(k):
            return rcopy(
                sendbuf.at[pl.ds(k * fold, fold)], stage, rl_s.at[k - 1], rl_r, row=k
            )

        def quarter(j):
            to = lax.rem(col + NX * j + row, ncol)
            src = stage.at[j]
            return rcopy(src, rq.at[col // NX], rq_s.at[j], rq_r.at[j], col=to)

        @pl.when(row == 0)
        def _():
            for k in (2, 1, 3):

                @pl.loop(0, fold)
                def _(j):
                    build(NX * j + k)

                lot_to(k).start()

            for k in (2, 1, 3):
                front_to(k).start()

            @pl.loop(0, fold)
            def _(j):
                build(NX * j)
                stage[j] = sendbuf[j]
                pl.when(j > 0)(lambda: quarter(j).start())

            rq[col // NX] = sendbuf[0]

        @pl.when(row != 0)
        def _():
            build(0)
            recv[0] = sendbuf[0]

            @pl.loop(1, ncol)
            def _(k):
                build(k)
                a2a(k).start()

        def pass_on():
            @pl.when((row > 0) & (row < NX))
            def _():
                lot_to(1).wait_recv()

                @pl.loop(0, fold)
                def _(j):
                    quarter(j).start()

        def share(k, to):
            n = lax.rem(to - k + 2 * NX, NX)
            return rcopy(pivots.at[:, lot(k)], pivots.at[:, lot(k)], rs_s.at[n], rs_r.at[k], row=to)

        def shares():
            x = lax.rem(row, NX)
            here = row - x
            return [share(x, here + lax.rem(x + d, NX)) for d in (2, 1, 3)]

        def cross():
            return share(row, row + NX)

        def gather_pivots():
            @pl.when(row < NX)
            def _():
                pl.when(row > 0)(lambda: front_to(1).wait_recv())

                @pl.loop(0, fold)
                def _(j):
                    pl.when((row > 0) | (j > 0))(lambda: quarter(j).wait_recv())

                m = lot(row)

                @pl.when(row == 0)
                def _():
                    pivots[:, m] = front[:, m] + rq[...]

                @pl.when(row > 0)
                def _():
                    pivots[:, m] = front_x[...] + rq[...]

                cross().start()
                start(shares())

        def fan_pivots():
            @pl.when(row >= NX)
            def _():
                share(row - NX, row).wait_recv()
                start(shares())

        d_own = y // (ny // 2) == other
        d_at = lax.rem(y, ny // 2)

        def d_out(k):
            ref = dbuf.at[leaf, d_at, z]
            return rcopy(ref, ref, d_s.at[k - 1], d_r, row=lax.rem(row + k, nrow))

        def d_first(which):
            ref = dbuf.at[which, d_at, z]
            return (over_y if which else over_z)(lambda t: ref, lambda i: ref, dg_s, dg_r)

        def d_second(which):
            ref = dbuf.at[1, :, z] if which else dbuf.at[0, d_at]
            return (over_z if which else over_y)(lambda t: ref, lambda i: ref, dh_s, dh_r)

        def d_slices(part):
            @pl.when(d_own & (row == 0))
            def _():
                dbuf[leaf, d_at, z] = part
                for k in range(1, nrow):
                    d_out(k).start()

        def d_spread(which):
            @pl.when(d_own)
            def _():
                pl.when(row > 0)(lambda: d_out(1).wait_recv())
                start(d_first(which))

        def y_arrive(copies):
            for d, cp in enumerate(copies, 1):
                pl.when(lax.rem(y - d + ny, ny) // (ny // 2) == other)(cp.wait_recv)

        def d_gather(which):
            if which:
                y_arrive(d_first(1))
                start(d_second(1))
            else:

                @pl.when(d_own)
                def _():
                    arrive(d_first(0))
                    start(d_second(0))

        def d_finish(which):
            if which:
                arrive(d_second(1))
            else:
                y_arrive(d_second(0))

        @each_leaf
        def _(which, steps):
            arrive(steps[0]())
            if which == 0:
                ysum[...] = colsum[y] + ybig[0] + ybig[1] + ybig[2]
            else:
                total = colsum[:, z]
                for d in range(NZ - 1):
                    total = total + zbig[d]
                zsum[...] = total
            start(steps[1]())

        pass_on()

        @each_leaf
        def _(which, steps):
            arrive(steps[1]())
            part, small, n = (ysum[z], zsmall, NZ - 1) if which == 0 else (zsum[y], ysmall, ny - 1)
            part = part + piece(2, which)
            for d in range(n):
                part = part + small[d]
            cb2[which, y, z] = part
            d_slices(part)
            start(steps[2]())
            d_spread(which)

        gather_pivots()

        @each_leaf
        def _(which, steps):
            arrive(steps[2]())
            start(steps[3]())
            d_gather(which)

        fan_pivots()

        @each_leaf
        def _(which, steps):
            arrive(steps[3]())
            d_finish(which)

        col_rc = rcopy(cb2.at[leaf], cb2.at[leaf], pair_s.at[2], pair_r.at[2], leaf=other)
        col_rc.start()
        d_rc = rcopy(dbuf.at[leaf], dbuf.at[leaf], pair_s.at[3], pair_r.at[3], leaf=other)
        d_rc.start()
        w_cp.wait()
        col_rc.wait_recv()
        d_rc.wait_recv()

        e[...] = dot3(w[0], dbuf[1].reshape(b, b))

        @pl.loop(0, ny // 2)
        def _(i):
            g[pl.ds(i * crow, crow), :] = dot3(dbuf[0, i].reshape(crow, b), w[0], True)

        @pl.loop(0, ny)
        def _(i):
            at = pl.ds(i * crow, crow)
            fa = dot3(cb2[0, i].reshape(crow, b), w[0], True)
            c1 = cb2[1, i].reshape(crow, b) - dot3(fa, e[...])
            fb = dot3(c1, w[1], True)
            f0[at, :] = jnp.where((row > 0) | (i >= ny // 2), fa, 0.0)
            f1[at, :] = jnp.where(row > 0, fb, 0.0)

        @pl.when(row != 0)
        def _():
            @pl.loop(0, ncol)
            def _(k):
                pl.when(k > 0)(lambda: a2a(k).wait_recv())
                at = back(k)
                work[at] = front[at // NX, lax.rem(at, NX)] + recv[k]

        for k in range(NX):
            pl.when((row != k) & (row != k + NX))(lambda k=k: share(k, row).wait_recv())

        @pl.when(row == 0)
        def _():
            @pl.loop(0, fold)
            def _(i):
                work[pl.ds(i * NX, NX)] = pivots[i]

        pr = b // sub // NX

        def out_copy(i):
            at = pl.ds(i * NZ, NZ)
            return pltpu.make_async_copy(work.at[at], out_h.at[at], out_sem.at[i])

        for t in range(2):
            lanes = slice(t * b, (t + 1) * b)
            pa = dot3(w[0], pivots[0:pr, :, :, lanes].reshape(b, b))
            zz = pivots[pr : 2 * pr, :, :, lanes].reshape(b, b) - dot3(g[...], pa)
            p0[:, lanes] = pa
            p1[:, lanes] = dot3(w[1], zz)
        @pl.loop(0, ny)
        def _(i):
            at = pl.ds(i * crow, crow)
            for t in range(2):
                lanes = slice(t * b, (t + 1) * b)
                s = 2 * own + t
                k0 = jnp.broadcast_to(pivot_slot[0], (crow, b)) != s
                k1 = k0 & (jnp.broadcast_to(pivot_slot[1], (crow, b)) != s)
                v = work[pl.ds(i * NZ, NZ), :, lanes].reshape(crow, b)
                v = v - jnp.where(k0, dot3(f0[at, :], p0[:, lanes]), 0.0)
                v = v - jnp.where(k1, dot3(f1[at, :], p1[:, lanes]), 0.0)
                work[pl.ds(i * NZ, NZ), :, lanes] = v.reshape(NZ, sub, b)
            out_copy(i).start()

        for cp in (child_rc, mask_rc, col_rc, d_rc):
            cp.wait_send()

        @each_leaf
        def _(which, steps):
            for step in steps:
                for cp in step():
                    cp.wait_send()

        @pl.when(row != 0)
        def _():
            @pl.loop(1, ncol)
            def _(k):
                a2a(k).wait_send()

        @pl.when(row == 0)
        def _():
            for k in range(1, NX):
                front_to(k).wait_send()
                lot_to(k).wait_send()

        @pl.when(row < NX)
        def _():
            @pl.loop(0, fold)
            def _(j):
                pl.when((row > 0) | (j > 0))(lambda: quarter(j).wait_send())

            cross().wait_send()

        for cp in shares():
            cp.wait_send()

        @pl.when(d_own & (row == 0))
        def _():
            for k in range(1, nrow):
                d_out(k).wait_send()

        @each_leaf
        def _(which, steps):
            @pl.when(d_own)
            def _():
                for cp in d_first(which):
                    cp.wait_send()

            if which:
                for cp in d_second(1):
                    cp.wait_send()
            else:

                @pl.when(d_own)
                def _():
                    for cp in d_second(0):
                        cp.wait_send()

        @pl.loop(0, ny)
        def _(i):
            out_copy(i).wait()

    dma = pltpu.SemaphoreType.DMA
    width = 2 * b
    rows = ncol * sub
    scratch = [
        pltpu.VMEM((2, sub, cb_count * b), F32),
        pltpu.VMEM((2 * cb_count, sub, b), F32),
        pltpu.VMEM((fold, NX, sub, width), F32),
        pltpu.VMEM((2, b, b), F32),
        pltpu.VMEM((ny, NZ, sub, b), F32),
        pltpu.VMEM((ny, NZ, sub, b), F32),
        pltpu.VMEM((ny, NZ, sub, b), F32),
        pltpu.VMEM((ny - 1, NZ, sub, b), F32),
        pltpu.VMEM((NZ, sub, b), F32),
        pltpu.VMEM((NZ - 1, sub, b), F32),
        pltpu.VMEM((NZ - 1, ny, sub, b), F32),
        pltpu.VMEM((ny, sub, b), F32),
        pltpu.VMEM((ny - 1, sub, b), F32),
        pltpu.VMEM((2, ny, NZ, sub, b), F32),
        pltpu.VMEM((2, ny // 2, NZ, sub, b), F32),
        pltpu.VMEM((ncol, sub, width), F32),
        pltpu.VMEM((ncol, sub, width), F32),
        pltpu.VMEM((ncol, sub, width), F32),
        pltpu.VMEM((fold, sub, width), F32),
        pltpu.VMEM((fold, sub, width), F32),
        pltpu.VMEM((fold, sub, width), F32),
        pltpu.VMEM((fold, NX, sub, width), F32),
        pltpu.VMEM((rows, b), F32),
        pltpu.VMEM((rows, b), F32),
        pltpu.VMEM((b, b), F32),
        pltpu.VMEM((b, b), F32),
        pltpu.VMEM((b, width), F32),
        pltpu.VMEM((b, width), F32),
        dma((4,)), dma((4,)), dma((4,)), dma((ncol,)), dma((ncol,)),
        dma((ny - 1,)), dma((ny - 1,)), dma((NZ - 1,)), dma((NZ - 1,)),
        dma((ny - 1,)), dma((ny - 1,)), dma((NZ - 1,)), dma((NZ - 1,)),
        dma((NX,)), dma((NX,)), dma((NX - 1,)), dma, dma((NX - 1,)), dma,
        dma((fold,)), dma((fold,)), dma((nrow - 1,)), dma,
        dma((NZ - 1,)), dma((NZ - 1,)), dma((NZ - 1,)), dma((NZ - 1,)), dma((ny,)),
    ]
    return kernel, scratch


def on_device(front, child_update, block_pattern, child_map, block_slot, diag_inverse):
    rows, width = front.shape
    b = diag_inverse.shape[1]
    sub = child_update.shape[1]
    nb = block_slot.shape[0]
    cb_count = child_map.shape[1]
    ncol, nrow = lax.axis_size("col"), lax.axis_size("row")
    kernel, scratch = make_kernel(ncol, nrow, b, nb, cb_count, sub)
    row_block = (lax.axis_index("row") * ncol + lax.axis_index("col")) * sub // b
    present = lax.dynamic_index_in_dim(block_pattern, row_block, 1, keepdims=False)
    code = (present * (jnp.arange(cb_count, dtype=jnp.int32) + 1))[:, :, None]
    ids = jnp.arange(nb, dtype=jnp.int32)
    parents = child_map[:, :, None]
    slots = jnp.sum(jnp.where(parents == ids, block_slot, 0), axis=2, keepdims=True)
    tables = jnp.concatenate(
        [jnp.sum(jnp.where(key == ids, code, 0), axis=1) for key in (slots, parents)]
    )
    hbm = pl.BlockSpec(memory_space=pl.ANY)
    vmem = pl.BlockSpec(memory_space=pltpu.VMEM)
    out = pl.pallas_call(
        kernel,
        out_shape=jax.ShapeDtypeStruct((ncol, sub, width), F32),
        in_specs=[hbm, hbm, hbm, pl.BlockSpec(memory_space=pltpu.SMEM), vmem],
        out_specs=hbm,
        scratch_shapes=scratch,
        compiler_params=pltpu.CompilerParams(
            collective_id=0, has_side_effects=True, vmem_limit_bytes=60 << 20
        ),
        cost_estimate=pl.CostEstimate(
            flops=6 * 22 * b * b * b, bytes_accessed=12 * rows * width, transcendentals=0
        ),
    )(
        child_update, front.reshape(ncol // NX, NX, sub, width), diag_inverse,
        tables, block_slot.reshape(1, nb),
    )
    return out.reshape(rows, width)


def solution(mesh):
    return jax.shard_map(
        on_device,
        mesh=mesh,
        in_specs=(P("row", ("leaf", "col")), P("leaf", ("row", "col"), None), P(), P(), P(), P()),
        out_specs=P("row", ("leaf", "col")),
        check_vma=False,
    )
```
